32 devices in a mesh: groups: 1, expert: 4 (over z), tensor: 4 (over y, x), seq: 2 (over core).
Axes of the slice: x: 2, y: 2, z: 4, core: 2. Of those that a mesh axis runs over, the one named last changes fastest.
Arguments:
- tokens: bfloat16 [2048, 2048], P(('groups', 'expert', 'seq'), 'tensor'), may hold values from -6 to 6
- expert_ids: int32 [2048, 8], P(('groups', 'expert', 'seq')), may hold values from 0 to 15, all different within a row; in each aligned block of 256 rows (0 to 255, 256 to 511, ...) at most 256 rows name the same one
- router_scores: float32 [2048, 8], P(('groups', 'expert', 'seq')), may hold values from 0.05 to 1
- w_gate: bfloat16 [16, 2048, 768], P(('expert', 'tensor'), None, 'seq'), may hold values from -0.125 to 0.125
- w_up: bfloat16 [16, 2048, 768], P(('expert', 'tensor'), None, 'seq'), may hold values from -0.125 to 0.125
- w_down: bfloat16 [16, 768, 2048], P(('expert', 'tensor'), 'seq'), may hold values from -0.21875 to 0.21875
Outputs:
- mixed: bfloat16 [2048, 2048], P(('groups', 'expert', 'seq'), 'tensor')
The draws below stay inside these ranges and needn't reach their ends.
Inputs may be any that keep to these rules, and one draw needn't show every extreme that they name: `expert_ids`: each row names 8 different experts. In each aligned block of 256 rows (the rows of one device) no expert is named by more than 256 rows, a bound that some block reaches.
All inputs are finite; a program needn't handle non-finite values.
Results may differ from the reference program's by a relative error of at most 0.0061.
Values may be sent and summed in bfloat16 or wider, within the bound.
A program may use at most 64 MiB of HBM per device.

```python
import math
import jax
import jax.numpy as jnp
import numpy as np
from jax import lax

D = 2048
FF = 768
TOP = 8
TOK_DEV = 256
EXPERTS = 16
TOKENS = 2048
CAP = 256


def level_of(rng, shape, split, least, largest):
    def one(dim, shards_of):
        steps = jax.random.uniform(jax.random.fold_in(jax.random.fold_in(rng, 6), dim), (shards_of,), jnp.float32, least / len(split), largest / len(split))
        return jnp.repeat(jnp.exp(steps), shape[dim] // shards_of).reshape((-1,) + (1,) * (len(shape) - dim - 1))

    factor_of = one(*split[0])
    for cut in split[1:]:
        factor_of = factor_of * one(*cut)
    return factor_of


def assign_block(stream_key, own, number, rows, count, top, limit, slope):
    order = jax.random.permutation(stream_key, count)
    packed, ordinary = portions_of(count, rows * top, limit, slope, True), portions_of(count, rows * top, limit, slope, False)
    places = jnp.arange(count)

    def named(tallies, turn):
        used = int((tallies > 0).sum())
        fixed = max(1, used // 4)
        moved = fixed + (places - fixed + turn * (used - fixed)) % max(1, count - fixed)
        return jnp.zeros((count,), jnp.int32).at[order[jnp.where(places < fixed, places, moved)]].set(jnp.asarray(tallies, jnp.int32))

    tallies = jnp.where(number % 4 == 0, named(packed, number // 4), named(ordinary, number - number // 4 - 1))
    mixed = jax.random.permutation(jax.random.fold_in(own, 3), count)
    donor, receiver = mixed[0:count // 2 * 2:2], mixed[1:count // 2 * 2:2]
    margin = jnp.minimum(tallies[donor] - 1, limit - tallies[receiver]) // 2
    margin = jnp.where((donor == order[0]) | (receiver == order[0]) | (tallies[receiver] == 0), 0, jnp.maximum(margin, 0))
    moved = jax.random.randint(jax.random.fold_in(own, 4), (count // 2,), 0, 1 << 20) % (margin + 1)
    tallies = tallies.at[donor].add(-moved).at[receiver].add(moved)
    items = jnp.searchsorted(jnp.cumsum(tallies), jnp.arange(rows * top), side="right").astype(jnp.int32)
    listing = items.reshape(top, rows).T
    listing = listing[jax.random.permutation(jax.random.fold_in(own, 1), rows)]
    turn = jax.random.randint(jax.random.fold_in(own, 2), (rows, 1), 0, top)
    return jnp.take_along_axis(listing, (jnp.arange(top)[None, :] + turn) % top, axis=1)


def portions_of(count, total, reach, skew, full):
    portions = [(1 << 20) // math.isqrt(rank ** skew) + 1 for rank in range(1, count + 1)]
    largest = reach if full else min(reach, max(-(-total // count), total * portions[0] // sum(portions)))
    least = 1 if total - largest >= count - 1 else 0
    counts, rest = [largest] + [least] * (count - 1), total - largest - least * (count - 1)
    while rest > 0:
        free = [i for i in range(1, count) if counts[i] < largest] or [i for i in range(1, count) if counts[i] < reach]
        pool, budget = sum([portions[i] for i in free]), rest
        for i in free:
            extra = min(reach - counts[i], max(1, budget * portions[i] // pool), rest)
            counts[i] = counts[i] + extra
            rest = rest - extra
    return np.array(counts)


def noise(stream_key, extent, scale, bound, pieces=(), kind=jnp.bfloat16):
    gain = level_of(stream_key, extent, pieces, -0.22, 0.18) if pieces else 1.0
    entries = jax.random.normal(stream_key, extent, jnp.float32) * scale * gain
    return jnp.minimum(jnp.maximum(entries, -bound), bound).astype(kind)


def setup_inputs(seed: int = 0, part: int = 0) -> dict:
    seeds = jax.random.split(jax.random.key(seed), 7)
    part_keys = jax.random.split(jax.random.fold_in(seeds[6], part), 7)
    tokens = noise(part_keys[0], (TOKENS, D), 1.0, 6.0, ((0, 8), (1, 4)))
    expert_ids_keys = jax.random.split(jax.random.fold_in(part_keys[1], 1), TOKENS // TOK_DEV)
    expert_ids_turns = jax.random.permutation(jax.random.fold_in(part_keys[1], 3), TOKENS // TOK_DEV)
    expert_ids = jax.vmap(lambda own, number: assign_block(jax.random.fold_in(part_keys[1], 2), own, number, TOK_DEV, EXPERTS, TOP, CAP, 2))(expert_ids_keys, expert_ids_turns).reshape((TOKENS, TOP))
    router_scores = jnp.clip(jnp.exp(math.log(1.0) - 2.9957323 * jax.random.uniform(part_keys[2], (TOKENS, TOP), jnp.float32) ** level_of(part_keys[2], (TOKENS, TOP), ((0, 8),), -0.2, 0.2)), 0.05, 1.0)
    w_gate = noise(seeds[3], (EXPERTS, D, FF), D ** -0.5, 0.125, ((0, 16), (2, 2)))
    w_up = noise(seeds[4], (EXPERTS, D, FF), D ** -0.5, 0.125, ((0, 16), (2, 2)))
    w_down = noise(seeds[5], (EXPERTS, FF, D), FF ** -0.5, 0.21875, ((0, 16), (1, 2)))
    return dict(tokens=tokens, expert_ids=expert_ids, router_scores=router_scores, w_gate=w_gate, w_up=w_up, w_down=w_down)


def reference(tokens, expert_ids, router_scores, w_gate, w_up, w_down):
    half = FF // 2
    most_rows = CAP * (TOKENS // TOK_DEV)
    flat_ids = expert_ids.reshape(-1)
    shares = (router_scores / jnp.sum(router_scores, axis=1, keepdims=True)).reshape(-1)

    def one_expert(total, inputs):
        number, gate_w, up_w, down_w = inputs
        chosen = flat_ids == number
        found = jnp.nonzero(chosen, size=most_rows, fill_value=0)[0].astype(jnp.int32)
        count = jnp.sum(chosen.astype(jnp.int32))
        live = jnp.arange(most_rows, dtype=jnp.int32) < count
        row = found // TOP
        block = tokens[row]
        gate = jnp.dot(block, gate_w, preferred_element_type=jnp.float32)
        upper = jnp.dot(block, up_w, preferred_element_type=jnp.float32)
        hidden = (jax.nn.silu(gate) * upper).astype(jnp.bfloat16)
        first = jnp.dot(hidden[:, :half], down_w[:half], preferred_element_type=jnp.float32)
        second = jnp.dot(hidden[:, half:], down_w[half:], preferred_element_type=jnp.float32)
        lower = ((row // TOK_DEV) % 2 == 0)[:, None]
        own = jnp.where(lower, first, second)
        far = jnp.where(lower, second, first)
        kept = lax.optimization_barrier(far.astype(jnp.bfloat16)).astype(jnp.float32)
        answer = (own + kept).astype(jnp.bfloat16)
        weight = jnp.where(live, shares[found], 0.0)
        total = total.at[row].add(answer.astype(jnp.float32) * weight[:, None])
        return total, None

    start = jnp.zeros((TOKENS, D), jnp.float32)
    numbers = jnp.arange(EXPERTS, dtype=jnp.int32)
    total, _ = lax.scan(one_expert, start, (numbers, w_gate, w_up, w_down))
    return total.astype(jnp.bfloat16)
```

```python
import jax
import jax.numpy as jnp
from jax import lax
from jax.sharding import PartitionSpec as P


def from_partner(value, axis, distance):
    mask = 2**distance
    pairs = [(source, source ^ mask) for source in range(lax.axis_size(axis))]
    return lax.ppermute(value, axis, pairs)


def expert_partial(block, gate_w, up_w, down_w):
    gate = jnp.einsum("...ecd,edf->...ecf", block, gate_w, preferred_element_type=jnp.float32)
    upper = jnp.einsum("...ecd,edf->...ecf", block, up_w, preferred_element_type=jnp.float32)
    hidden = (jax.nn.silu(gate) * upper).astype(jnp.bfloat16)
    return jnp.einsum("...ecf,efd->...ecd", hidden, down_w, preferred_element_type=jnp.float32)


def round_half(values):
    kept = lax.optimization_barrier(values.astype(jnp.bfloat16))
    return kept.astype(jnp.float32)


def slot_positions(keys, count):
    onehot = (keys[:, None] == jnp.arange(count, dtype=jnp.int32)[None, :]).astype(jnp.int32)
    before = jnp.cumsum(onehot, axis=0) - onehot
    return jnp.sum(before * onehot, axis=1)


def body(tokens, expert_ids, router_scores, w_gate, w_up, w_down):
    tok_rows, top = expert_ids.shape
    exp_dev = w_gate.shape[0]
    n_owner = lax.axis_size("expert")
    n_tensor = lax.axis_size("tensor")
    experts_all = exp_dev * n_owner * n_tensor
    slots = min(tok_rows, max(2, tok_rows * top * 2 // experts_all))
    buckets = n_owner * exp_dev
    shares = router_scores / jnp.sum(router_scores, axis=1, keepdims=True)
    flat_ids = expert_ids.reshape(-1)
    source_row = jnp.arange(tok_rows * top, dtype=jnp.int32) // top
    whole = lax.all_gather(tokens, "tensor", axis=1, tiled=True)
    column = lax.axis_index("tensor")
    mine = flat_ids // exp_dev % n_tensor == column
    bucket = flat_ids // (exp_dev * n_tensor) * exp_dev + flat_ids % exp_dev
    masked = jnp.where(mine, bucket, buckets)
    position = slot_positions(masked, buckets)
    target = jnp.where(mine, bucket * slots + position, buckets * slots)
    width = whole.shape[1]
    outgoing = (
        jnp.zeros((buckets * slots + 1, width), jnp.bfloat16).at[target].set(whole[source_row])
    )
    outgoing = outgoing[: buckets * slots].reshape(n_owner, exp_dev, slots, width)
    arrived = lax.all_to_all(outgoing, "expert", split_axis=0, concat_axis=0, tiled=True)
    other_gate, other_up, other_down = from_partner((w_gate, w_up, w_down), "seq", 0)
    own_part = expert_partial(arrived, w_gate, w_up, w_down)
    far_part = expert_partial(arrived, other_gate, other_up, other_down)
    answer = (own_part + round_half(far_part)).astype(jnp.bfloat16)
    back = lax.all_to_all(answer, "expert", split_axis=0, concat_axis=0, tiled=True)
    width = back.shape[-1]
    flat_back = jnp.concatenate(
        [back.reshape(buckets * slots, width), jnp.zeros((1, width), jnp.bfloat16)], axis=0
    )
    picked = flat_back[target].reshape(tok_rows, top, width)
    share_mine = jnp.where(mine.reshape(tok_rows, top), shares, 0.0)
    combined = jnp.sum(picked.astype(jnp.float32) * share_mine[:, :, None], axis=1)
    return lax.psum_scatter(combined, "tensor", scatter_dimension=1, tiled=True).astype(
        jnp.bfloat16
    )


def dense_body(tokens, expert_ids, router_scores, w_gate, w_up, w_down):
    tok_rows, top = expert_ids.shape
    n_tensor = lax.axis_size("tensor")
    shares = router_scores / jnp.sum(router_scores, axis=1, keepdims=True)
    number = jnp.arange(lax.axis_size("expert") * n_tensor, dtype=jnp.int32)
    table = jnp.sum(
        jnp.where(expert_ids[:, :, None] == number, shares[:, :, None], 0.0), axis=1
    )
    tables = lax.all_gather(table, "expert", axis=0, tiled=True)
    expert = lax.axis_index("expert") * n_tensor + lax.axis_index("tensor")
    weight = jnp.sum(jnp.where(number == expert, tables, 0.0), axis=1)
    other_gate, other_up, other_down = from_partner((w_gate, w_up, w_down), "seq", 0)
    rows = lax.all_gather(tokens, "expert", axis=0, tiled=True)
    whole = lax.all_gather(rows, "tensor", axis=1, tiled=True)[None]
    own_part = expert_partial(whole, w_gate, w_up, w_down)
    far_part = expert_partial(whole, other_gate, other_up, other_down)
    answer = ((own_part + far_part)[0] * weight[:, None]).astype(jnp.bfloat16)
    part = lax.psum_scatter(answer, "tensor", scatter_dimension=1, tiled=True)
    return lax.psum_scatter(part, "expert", scatter_dimension=0, tiled=True)


def pick_body(tokens, expert_ids, router_scores, w_gate, w_up, w_down):
    tok_rows, top = expert_ids.shape
    exp_dev = w_gate.shape[0]
    experts_all = exp_dev * lax.axis_size("expert") * lax.axis_size("tensor")
    slots = min(tok_rows, max(2, tok_rows * top * 2 // experts_all))
    plan = dense_body if exp_dev == 1 and slots == tok_rows else body
    return plan(tokens, expert_ids, router_scores, w_gate, w_up, w_down)


def solution(mesh):
    placed = (
        P(("groups", "expert", "seq"), "tensor"),
        P(("groups", "expert", "seq"), None),
        P(("groups", "expert", "seq"), None),
        P(("expert", "tensor"), None, "seq"),
        P(("expert", "tensor"), None, "seq"),
        P(("expert", "tensor"), "seq", None),
    )
    return jax.shard_map(
        pick_body,
        mesh=mesh,
        in_specs=placed,
        out_specs=P(("groups", "expert", "seq"), "tensor"),
        check_vma=False,
    )
```

```python
import jax
import jax.numpy as jnp
from jax import lax
from jax.experimental import pallas as pl
from jax.experimental.pallas import tpu as pltpu
from jax.sharding import PartitionSpec as P


def from_partner(value, axis, distance):
    mask = 2**distance
    pairs = [(source, source ^ mask) for source in range(lax.axis_size(axis))]
    return lax.ppermute(value, axis, pairs)


def expert_partial(block, gate_w, up_w, down_w):
    gate = jnp.einsum("...ecd,edf->...ecf", block, gate_w, preferred_element_type=jnp.float32)
    upper = jnp.einsum("...ecd,edf->...ecf", block, up_w, preferred_element_type=jnp.float32)
    hidden = (jax.nn.silu(gate) * upper).astype(jnp.bfloat16)
    return jnp.einsum("...ecf,efd->...ecd", hidden, down_w, preferred_element_type=jnp.float32)


def round_half(values):
    kept = lax.optimization_barrier(values.astype(jnp.bfloat16))
    return kept.astype(jnp.float32)


def slot_positions(keys, count):
    onehot = (keys[:, None] == jnp.arange(count, dtype=jnp.int32)[None, :]).astype(jnp.int32)
    before = jnp.cumsum(onehot, axis=0) - onehot
    return jnp.sum(before * onehot, axis=1)


def body(tokens, expert_ids, router_scores, w_gate, w_up, w_down):
    tok_rows, top = expert_ids.shape
    exp_dev = w_gate.shape[0]
    n_owner = lax.axis_size("expert")
    n_tensor = lax.axis_size("tensor")
    experts_all = exp_dev * n_owner * n_tensor
    slots = min(tok_rows, max(2, tok_rows * top * 2 // experts_all))
    buckets = n_owner * exp_dev
    shares = router_scores / jnp.sum(router_scores, axis=1, keepdims=True)
    flat_ids = expert_ids.reshape(-1)
    source_row = jnp.arange(tok_rows * top, dtype=jnp.int32) // top
    whole = lax.all_gather(tokens, "tensor", axis=1, tiled=True)
    column = lax.axis_index("tensor")
    mine = flat_ids // exp_dev % n_tensor == column
    bucket = flat_ids // (exp_dev * n_tensor) * exp_dev + flat_ids % exp_dev
    masked = jnp.where(mine, bucket, buckets)
    position = slot_positions(masked, buckets)
    target = jnp.where(mine, bucket * slots + position, buckets * slots)
    width = whole.shape[1]
    outgoing = (
        jnp.zeros((buckets * slots + 1, width), jnp.bfloat16).at[target].set(whole[source_row])
    )
    outgoing = outgoing[: buckets * slots].reshape(n_owner, exp_dev, slots, width)
    arrived = lax.all_to_all(outgoing, "expert", split_axis=0, concat_axis=0, tiled=True)
    other_gate, other_up, other_down = from_partner((w_gate, w_up, w_down), "seq", 0)
    own_part = expert_partial(arrived, w_gate, w_up, w_down)
    far_part = expert_partial(arrived, other_gate, other_up, other_down)
    answer = (own_part + round_half(far_part)).astype(jnp.bfloat16)
    back = lax.all_to_all(answer, "expert", split_axis=0, concat_axis=0, tiled=True)
    width = back.shape[-1]
    flat_back = jnp.concatenate(
        [back.reshape(buckets * slots, width), jnp.zeros((1, width), jnp.bfloat16)], axis=0
    )
    picked = flat_back[target].reshape(tok_rows, top, width)
    share_mine = jnp.where(mine.reshape(tok_rows, top), shares, 0.0)
    combined = jnp.sum(picked.astype(jnp.float32) * share_mine[:, :, None], axis=1)
    return lax.psum_scatter(combined, "tensor", scatter_dimension=1, tiled=True).astype(
        jnp.bfloat16
    )


def dense_kernel(
    tokens, table, gate_w, up_w, down_w, out,
    rows, tables, gate_all, up_all, down_all, hidden, part,
    diag, joined, side, final, back, send, recv, local,
):
    n_rows, cols = tokens.shape
    half = n_rows // 2
    units = gate_w.shape[2]
    z = lax.axis_index("expert")
    t = lax.axis_index("tensor")
    s = lax.axis_index("seq")
    tx, ty, td = t + 1 - 2 * (t % 2), (t + 2) % 4, 3 - t
    beside = ({"tensor": tx}, {"tensor": ty})
    along = (None, {"expert": z + 1 - 2 * (z % 2)}, {"expert": (z + 2) % 4}, {"expert": 3 - z})
    partner = {"seq": 1 - s}
    low, high, full = pl.ds(0, half), pl.ds(half, half), pl.ds(0, n_rows)

    def span(index):
        return pl.ds(pl.multiple_of(index * cols, cols), cols)

    barrier = pltpu.get_barrier_semaphore()
    for device in (partner,) + beside + along[1:]:
        pl.semaphore_signal(barrier, inc=1, device_id=device, device_id_type=pl.DeviceIdType.MESH)
    pl.semaphore_wait(barrier, 6)

    def remote(source, target, number, device):
        return pltpu.make_async_remote_copy(
            src_ref=source,
            dst_ref=target,
            send_sem=send.at[number],
            recv_sem=recv.at[number],
            device_id=device,
            device_id_type=pl.DeviceIdType.MESH,
        )

    mine = span(t)
    to_z = [None] + [remote(tokens, rows.at[j, :, mine], 2 + j, along[j]) for j in (1, 2, 3)]
    table_z = [None] + [remote(table, tables.at[j], 5 + j, along[j]) for j in (1, 2, 3)]
    direct, passed, ahead, plain, summed = [], [], [], [], []
    for j in range(4):
        block = rows.at[j, :, mine]
        origin = tokens if j == 0 else block
        direct.append([remote(origin, block, 9 + 2 * j + d, beside[d]) for d in (0, 1)])
        passed.append([
            remote(rows.at[j, high, span(ty)], rows.at[j, high, span(ty)], 17 + 2 * j, beside[0]),
            remote(rows.at[j, low, span(tx)], rows.at[j, low, span(tx)], 18 + 2 * j, beside[1]),
        ])
        ahead.append([
            remote(part.at[j, low, span(td)], diag.at[j, 0], 25 + 2 * j, beside[0]),
            remote(part.at[j, high, span(td)], diag.at[j, 1], 26 + 2 * j, beside[1]),
        ])
        plain.append([
            remote(part.at[j, low, span(tx)], side.at[j, 0, low], 33 + 2 * j, beside[0]),
            remote(part.at[j, high, span(ty)], side.at[j, 1, high], 34 + 2 * j, beside[1]),
        ])
        summed.append([
            remote(joined.at[j, 0], side.at[j, 0, high], 41 + 2 * j, beside[0]),
            remote(joined.at[j, 1], side.at[j, 1, low], 42 + 2 * j, beside[1]),
        ])
    to_home = [None] + [remote(final.at[j], back.at[j], 48 + j, along[j]) for j in (1, 2, 3)]
    weights = [
        remote(gate_w.at[0], gate_all.at[:, pl.ds(units, units)], 0, partner),
        remote(up_w.at[0], up_all.at[:, pl.ds(units, units)], 1, partner),
        remote(down_w.at[0], down_all.at[pl.ds(units, units)], 2, partner),
    ]
    loads = [
        pltpu.make_async_copy(tokens, rows.at[0, :, mine], local.at[0]),
        pltpu.make_async_copy(gate_w.at[0], gate_all.at[:, pl.ds(0, units)], local.at[1]),
        pltpu.make_async_copy(up_w.at[0], up_all.at[:, pl.ds(0, units)], local.at[2]),
        pltpu.make_async_copy(down_w.at[0], down_all.at[pl.ds(0, units)], local.at[3]),
        pltpu.make_async_copy(table, tables.at[0], local.at[4]),
    ]

    def start(copies):
        for copy in copies:
            copy.start()

    def arrive(copies):
        for copy in copies:
            copy.wait_recv()

    def spread(j):
        to_z[j].wait_recv()
        start(direct[j])

    def pass_on(j):
        arrive(direct[j])
        start(passed[j])

    def answer(j, sending):
        arrive(passed[j])

        def inner(c, carry):
            at = pl.ds(pl.multiple_of(c * 256, 256), 256)
            gate = jnp.dot(rows[j], gate_all[:, at], preferred_element_type=jnp.float32)
            upper = jnp.dot(rows[j], up_all[:, at], preferred_element_type=jnp.float32)
            hidden[:, at] = (gate * jax.nn.sigmoid(gate) * upper).astype(jnp.bfloat16)
            return carry

        lax.fori_loop(0, 2 * units // 256, inner, 0)
        share = tables[j, pl.ds(z * 4 + t, 1), :]
        share = jnp.broadcast_to(share, (128, n_rows)).T[:, :1]
        for index, copies in ((td, ahead[j]), (tx, plain[j][:1]), (ty, plain[j][1:]), (t, [])):
            value = jnp.dot(hidden[...], down_all[:, span(index)], preferred_element_type=jnp.float32)
            part[j, :, span(index)] = (value * share).astype(jnp.bfloat16)
            if sending:
                start(copies)

    def join(j):
        arrive(ahead[j])
        upper_rows = part[j, high, span(tx)].astype(jnp.float32) + diag[j, 1].astype(jnp.float32)
        joined[j, 0] = upper_rows.astype(jnp.bfloat16)
        lower_rows = part[j, low, span(ty)].astype(jnp.float32) + diag[j, 0].astype(jnp.float32)
        joined[j, 1] = lower_rows.astype(jnp.bfloat16)
        start(summed[j])

    def gathered(j):
        arrive(plain[j] + summed[j])
        return (
            part[j, :, mine].astype(jnp.float32)
            + side[j, 0].astype(jnp.float32)
            + side[j, 1].astype(jnp.float32)
        )

    def go_home(j):
        final[j] = gathered(j).astype(jnp.bfloat16)
        to_home[j].start()

    start(direct[0])
    start(to_z[1:])
    start(table_z[1:])
    start(weights)
    start(loads)
    spread(1)
    pass_on(0)
    spread(2)
    for copy in loads:
        copy.wait()
    arrive(weights + table_z[1:])
    answer(0, False)
    pass_on(1)
    spread(3)
    answer(1, True)
    pass_on(2)
    answer(2, True)
    join(1)
    pass_on(3)
    start(ahead[0] + plain[0])
    answer(3, True)
    join(2)
    go_home(1)
    join(3)
    go_home(2)
    join(0)
    go_home(3)
    total = gathered(0)
    arrive(to_home[1:])
    for j in (1, 2, 3):
        total = total + back[j].astype(jnp.float32)
    out[...] = total.astype(jnp.bfloat16)
    everything = to_z[1:] + table_z[1:] + weights + to_home[1:]
    for group in direct + passed + ahead + plain + summed:
        everything = everything + group
    for copy in everything:
        copy.wait_send()


def dense_body(tokens, expert_ids, router_scores, w_gate, w_up, w_down):
    n_rows, cols = tokens.shape
    _, width, units = w_gate.shape
    half = n_rows // 2
    shares = router_scores / jnp.sum(router_scores, axis=1, keepdims=True)
    number = jnp.arange(16, dtype=jnp.int32)[:, None, None]
    table = jnp.sum(jnp.where(expert_ids.T[None] == number, shares.T[None], 0.0), axis=1)
    bf16 = jnp.bfloat16
    return pl.pallas_call(
        dense_kernel,
        out_shape=jax.ShapeDtypeStruct((n_rows, cols), bf16),
        in_specs=[pl.BlockSpec(memory_space=pl.ANY)] * 5,
        out_specs=pl.BlockSpec(memory_space=pltpu.VMEM),
        scratch_shapes=[
            pltpu.VMEM((4, n_rows, width), bf16),
            pltpu.VMEM((4, 16, n_rows), jnp.float32),
            pltpu.VMEM((width, 2 * units), bf16),
            pltpu.VMEM((width, 2 * units), bf16),
            pltpu.VMEM((2 * units, width), bf16),
            pltpu.VMEM((n_rows, 2 * units), bf16),
            pltpu.VMEM((4, n_rows, width), bf16),
            pltpu.VMEM((4, 2, half, cols), bf16),
            pltpu.VMEM((4, 2, half, cols), bf16),
            pltpu.VMEM((4, 2, n_rows, cols), bf16),
            pltpu.VMEM((4, n_rows, cols), bf16),
            pltpu.VMEM((4, n_rows, cols), bf16),
            pltpu.SemaphoreType.DMA((52,)),
            pltpu.SemaphoreType.DMA((52,)),
            pltpu.SemaphoreType.DMA((5,)),
        ],
        compiler_params=pltpu.CompilerParams(
            collective_id=0, has_side_effects=True, vmem_limit_bytes=44 * 1024 * 1024
        ),
        cost_estimate=pl.CostEstimate(
            flops=4 * n_rows * 6 * width * 2 * units,
            bytes_accessed=6 * width * units * 2,
            transcendentals=4 * n_rows * 2 * units,
        ),
    )(tokens, table, w_gate, w_up, w_down)


def pick_body(tokens, expert_ids, router_scores, w_gate, w_up, w_down):
    tok_rows, top = expert_ids.shape
    exp_dev = w_gate.shape[0]
    n_owner, n_tensor = lax.axis_size("expert"), lax.axis_size("tensor")
    slots = min(tok_rows, max(2, tok_rows * top * 2 // (exp_dev * n_owner * n_tensor)))
    dense = exp_dev == 1 and n_owner == 4 and n_tensor == 4 and slots == tok_rows
    plan = dense_body if dense else body
    return plan(tokens, expert_ids, router_scores, w_gate, w_up, w_down)


def solution(mesh):
    placed = (
        P(("groups", "expert", "seq"), "tensor"),
        P(("groups", "expert", "seq"), None),
        P(("groups", "expert", "seq"), None),
        P(("expert", "tensor"), None, "seq"),
        P(("expert", "tensor"), None, "seq"),
        P(("expert", "tensor"), "seq", None),
    )
    return jax.shard_map(
        pick_body,
        mesh=mesh,
        in_specs=placed,
        out_specs=P(("groups", "expert", "seq"), "tensor"),
        check_vma=False,
    )
```

```python
import jax
import jax.numpy as jnp
from jax import lax
from jax.experimental import pallas as pl
from jax.experimental.pallas import tpu as pltpu
from jax.sharding import PartitionSpec as P


def from_partner(value, axis, distance):
    mask = 2**distance
    pairs = [(source, source ^ mask) for source in range(lax.axis_size(axis))]
    return lax.ppermute(value, axis, pairs)


def expert_partial(block, gate_w, up_w, down_w):
    gate = jnp.einsum("...ecd,edf->...ecf", block, gate_w, preferred_element_type=jnp.float32)
    upper = jnp.einsum("...ecd,edf->...ecf", block, up_w, preferred_element_type=jnp.float32)
    hidden = (jax.nn.silu(gate) * upper).astype(jnp.bfloat16)
    return jnp.einsum("...ecf,efd->...ecd", hidden, down_w, preferred_element_type=jnp.float32)


def round_half(values):
    kept = lax.optimization_barrier(values.astype(jnp.bfloat16))
    return kept.astype(jnp.float32)


def slot_positions(keys, count):
    onehot = (keys[:, None] == jnp.arange(count, dtype=jnp.int32)[None, :]).astype(jnp.int32)
    before = jnp.cumsum(onehot, axis=0) - onehot
    return jnp.sum(before * onehot, axis=1)


def body(tokens, expert_ids, router_scores, w_gate, w_up, w_down):
    tok_rows, top = expert_ids.shape
    exp_dev = w_gate.shape[0]
    n_owner = lax.axis_size("expert")
    n_tensor = lax.axis_size("tensor")
    experts_all = exp_dev * n_owner * n_tensor
    slots = min(tok_rows, max(2, tok_rows * top * 2 // experts_all))
    buckets = n_owner * exp_dev
    shares = router_scores / jnp.sum(router_scores, axis=1, keepdims=True)
    flat_ids = expert_ids.reshape(-1)
    source_row = jnp.arange(tok_rows * top, dtype=jnp.int32) // top
    whole = lax.all_gather(tokens, "tensor", axis=1, tiled=True)
    column = lax.axis_index("tensor")
    mine = flat_ids // exp_dev % n_tensor == column
    bucket = flat_ids // (exp_dev * n_tensor) * exp_dev + flat_ids % exp_dev
    masked = jnp.where(mine, bucket, buckets)
    position = slot_positions(masked, buckets)
    target = jnp.where(mine, bucket * slots + position, buckets * slots)
    width = whole.shape[1]
    outgoing = (
        jnp.zeros((buckets * slots + 1, width), jnp.bfloat16).at[target].set(whole[source_row])
    )
    outgoing = outgoing[: buckets * slots].reshape(n_owner, exp_dev, slots, width)
    arrived = lax.all_to_all(outgoing, "expert", split_axis=0, concat_axis=0, tiled=True)
    other_gate, other_up, other_down = from_partner((w_gate, w_up, w_down), "seq", 0)
    own_part = expert_partial(arrived, w_gate, w_up, w_down)
    far_part = expert_partial(arrived, other_gate, other_up, other_down)
    answer = (own_part + round_half(far_part)).astype(jnp.bfloat16)
    back = lax.all_to_all(answer, "expert", split_axis=0, concat_axis=0, tiled=True)
    width = back.shape[-1]
    flat_back = jnp.concatenate(
        [back.reshape(buckets * slots, width), jnp.zeros((1, width), jnp.bfloat16)], axis=0
    )
    picked = flat_back[target].reshape(tok_rows, top, width)
    share_mine = jnp.where(mine.reshape(tok_rows, top), shares, 0.0)
    combined = jnp.sum(picked.astype(jnp.float32) * share_mine[:, :, None], axis=1)
    return lax.psum_scatter(combined, "tensor", scatter_dimension=1, tiled=True).astype(
        jnp.bfloat16
    )


def dense_kernel(
    tokens, table, gate_w, up_w, down_w, out,
    rows, tables, gate_all, up_all, down_all, hidden, part,
    diag, joined, side, final, back, send, recv, local,
):
    n_rows, cols = tokens.shape
    half = n_rows // 2
    units = gate_w.shape[2]
    z = lax.axis_index("expert")
    t = lax.axis_index("tensor")
    s = lax.axis_index("seq")
    tx, ty, td = t + 1 - 2 * (t % 2), (t + 2) % 4, 3 - t
    beside = ({"tensor": tx}, {"tensor": ty})
    along = (None, {"expert": z + 1 - 2 * (z % 2)}, {"expert": (z + 2) % 4}, {"expert": 3 - z})
    partner = {"seq": 1 - s}
    low, high, full = pl.ds(0, half), pl.ds(half, half), pl.ds(0, n_rows)

    def span(index):
        return pl.ds(pl.multiple_of(index * cols, cols), cols)

    barrier = pltpu.get_barrier_semaphore()
    for device in (partner,) + beside + along[1:]:
        pl.semaphore_signal(barrier, inc=1, device_id=device, device_id_type=pl.DeviceIdType.MESH)
    pl.semaphore_wait(barrier, 6)

    def remote(source, target, number, device):
        return pltpu.make_async_remote_copy(
            src_ref=source,
            dst_ref=target,
            send_sem=send.at[number],
            recv_sem=recv.at[number],
            device_id=device,
            device_id_type=pl.DeviceIdType.MESH,
        )

    mine = span(t)
    to_z = [None] + [remote(tokens, rows.at[j, :, mine], 2 + j, along[j]) for j in (1, 2, 3)]
    table_z = [None] + [remote(table, tables.at[j], 5 + j, along[j]) for j in (1, 2, 3)]
    direct, passed, ahead, plain, summed = [], [], [], [], []
    for j in range(4):
        block = rows.at[j, :, mine]
        origin = tokens if j == 0 else block
        direct.append([remote(origin, block, 9 + 2 * j + d, beside[d]) for d in (0, 1)])
        passed.append([
            remote(rows.at[j, high, span(ty)], rows.at[j, high, span(ty)], 17 + 2 * j, beside[0]),
            remote(rows.at[j, low, span(tx)], rows.at[j, low, span(tx)], 18 + 2 * j, beside[1]),
        ])
        ahead.append([
            remote(part.at[j, low, span(td)], diag.at[j, 0], 25 + 2 * j, beside[0]),
            remote(part.at[j, high, span(td)], diag.at[j, 1], 26 + 2 * j, beside[1]),
        ])
        plain.append([
            remote(part.at[j, low, span(tx)], side.at[j, 0, low], 33 + 2 * j, beside[0]),
            remote(part.at[j, high, span(ty)], side.at[j, 1, high], 34 + 2 * j, beside[1]),
        ])
        summed.append([
            remote(joined.at[j, 0], side.at[j, 0, high], 41 + 2 * j, beside[0]),
            remote(joined.at[j, 1], side.at[j, 1, low], 42 + 2 * j, beside[1]),
        ])
    relay = [
        remote(rows.at[0, :, span(index)], rows.at[1, :, span(index)], 52 + i, along[1])
        for i, index in enumerate((tx, ty, td))
    ]
    to_home = [None] + [remote(final.at[j], back.at[j], 48 + j, along[j]) for j in (1, 2, 3)]
    weights = [
        remote(gate_w.at[0], gate_all.at[:, pl.ds(units, units)], 0, partner),
        remote(up_w.at[0], up_all.at[:, pl.ds(units, units)], 1, partner),
        remote(down_w.at[0], down_all.at[pl.ds(units, units)], 2, partner),
    ]
    loads = [
        pltpu.make_async_copy(tokens, rows.at[0, :, mine], local.at[0]),
        pltpu.make_async_copy(gate_w.at[0], gate_all.at[:, pl.ds(0, units)], local.at[1]),
        pltpu.make_async_copy(up_w.at[0], up_all.at[:, pl.ds(0, units)], local.at[2]),
        pltpu.make_async_copy(down_w.at[0], down_all.at[pl.ds(0, units)], local.at[3]),
        pltpu.make_async_copy(table, tables.at[0], local.at[4]),
    ]

    def start(copies):
        for copy in copies:
            copy.start()

    def arrive(copies):
        for copy in copies:
            copy.wait_recv()

    def spread(j):
        to_z[j].wait_recv()
        start(direct[j])

    def pass_on(j):
        arrive(direct[j])
        start(passed[j])
        if j == 0:
            start(relay[:2])

    def answer(j, sending):
        arrive(to_z[1:2] + relay if j == 1 else passed[j])
        if j == 0:
            start(relay[2:])

        def inner(c, carry):
            at = pl.ds(pl.multiple_of(c * 256, 256), 256)
            gate = jnp.dot(rows[j], gate_all[:, at], preferred_element_type=jnp.float32)
            upper = jnp.dot(rows[j], up_all[:, at], preferred_element_type=jnp.float32)
            hidden[:, at] = (gate * jax.nn.sigmoid(gate) * upper).astype(jnp.bfloat16)
            return carry

        lax.fori_loop(0, 2 * units // 256, inner, 0)
        share = tables[j, pl.ds(z * 4 + t, 1), :]
        share = jnp.broadcast_to(share, (128, n_rows)).T[:, :1]
        for index, copies in ((td, ahead[j]), (tx, plain[j][:1]), (ty, plain[j][1:]), (t, [])):
            value = jnp.dot(hidden[...], down_all[:, span(index)], preferred_element_type=jnp.float32)
            part[j, :, span(index)] = (value * share).astype(jnp.bfloat16)
            if sending:
                start(copies)

    def join(j):
        arrive(ahead[j])
        upper_rows = part[j, high, span(tx)].astype(jnp.float32) + diag[j, 1].astype(jnp.float32)
        joined[j, 0] = upper_rows.astype(jnp.bfloat16)
        lower_rows = part[j, low, span(ty)].astype(jnp.float32) + diag[j, 0].astype(jnp.float32)
        joined[j, 1] = lower_rows.astype(jnp.bfloat16)
        start(summed[j])

    def gathered(j):
        arrive(plain[j] + summed[j])
        return (
            part[j, :, mine].astype(jnp.float32)
            + side[j, 0].astype(jnp.float32)
            + side[j, 1].astype(jnp.float32)
        )

    def go_home(j):
        final[j] = gathered(j).astype(jnp.bfloat16)
        to_home[j].start()

    start(direct[0])
    start(to_z[2:] + to_z[1:2])
    start(table_z[1:])
    start(weights)
    start(loads)
    pass_on(0)
    spread(2)
    for copy in loads:
        copy.wait()
    arrive(weights + table_z[1:])
    answer(0, False)
    pass_on(2)
    spread(3)
    answer(2, True)
    pass_on(3)
    answer(3, True)
    join(2)
    start(ahead[0] + plain[0])
    answer(1, True)
    join(3)
    go_home(2)
    join(1)
    go_home(3)
    join(0)
    go_home(1)
    total = gathered(0)
    arrive(to_home[1:])
    for j in (1, 2, 3):
        total = total + back[j].astype(jnp.float32)
    out[...] = total.astype(jnp.bfloat16)
    everything = to_z[1:] + relay + table_z[1:] + weights + to_home[1:]
    for group in direct[:1] + direct[2:] + passed[:1] + passed[2:] + ahead + plain + summed:
        everything = everything + group
    for copy in everything:
        copy.wait_send()


def dense_body(tokens, expert_ids, router_scores, w_gate, w_up, w_down):
    n_rows, cols = tokens.shape
    _, width, units = w_gate.shape
    half = n_rows // 2
    shares = router_scores / jnp.sum(router_scores, axis=1, keepdims=True)
    number = jnp.arange(16, dtype=jnp.int32)[:, None, None]
    table = jnp.sum(jnp.where(expert_ids.T[None] == number, shares.T[None], 0.0), axis=1)
    bf16 = jnp.bfloat16
    return pl.pallas_call(
        dense_kernel,
        out_shape=jax.ShapeDtypeStruct((n_rows, cols), bf16),
        in_specs=[pl.BlockSpec(memory_space=pltpu.HBM)] * 5,
        out_specs=pl.BlockSpec(memory_space=pltpu.VMEM),
        scratch_shapes=[
            pltpu.VMEM((4, n_rows, width), bf16),
            pltpu.VMEM((4, 16, n_rows), jnp.float32),
            pltpu.VMEM((width, 2 * units), bf16),
            pltpu.VMEM((width, 2 * units), bf16),
            pltpu.VMEM((2 * units, width), bf16),
            pltpu.VMEM((n_rows, 2 * units), bf16),
            pltpu.VMEM((4, n_rows, width), bf16),
            pltpu.VMEM((4, 2, half, cols), bf16),
            pltpu.VMEM((4, 2, half, cols), bf16),
            pltpu.VMEM((4, 2, n_rows, cols), bf16),
            pltpu.VMEM((4, n_rows, cols), bf16),
            pltpu.VMEM((4, n_rows, cols), bf16),
            pltpu.SemaphoreType.DMA((55,)),
            pltpu.SemaphoreType.DMA((55,)),
            pltpu.SemaphoreType.DMA((5,)),
        ],
        compiler_params=pltpu.CompilerParams(
            collective_id=0, has_side_effects=True, vmem_limit_bytes=62 * 1024 * 1024
        ),
        cost_estimate=pl.CostEstimate(
            flops=4 * n_rows * 6 * width * 2 * units,
            bytes_accessed=6 * width * units * 2,
            transcendentals=4 * n_rows * 2 * units,
        ),
    )(tokens, table, w_gate, w_up, w_down)


def pick_body(tokens, expert_ids, router_scores, w_gate, w_up, w_down):
    tok_rows, top = expert_ids.shape
    exp_dev = w_gate.shape[0]
    n_owner, n_tensor = lax.axis_size("expert"), lax.axis_size("tensor")
    slots = min(tok_rows, max(2, tok_rows * top * 2 // (exp_dev * n_owner * n_tensor)))
    dense = exp_dev == 1 and n_owner == 4 and n_tensor == 4 and slots == tok_rows
    plan = dense_body if dense else body
    return plan(tokens, expert_ids, router_scores, w_gate, w_up, w_down)


def solution(mesh):
    placed = (
        P(("groups", "expert", "seq"), "tensor"),
        P(("groups", "expert", "seq"), None),
        P(("groups", "expert", "seq"), None),
        P(("expert", "tensor"), None, "seq"),
        P(("expert", "tensor"), None, "seq"),
        P(("expert", "tensor"), "seq", None),
    )
    return jax.shard_map(
        pick_body,
        mesh=mesh,
        in_specs=placed,
        out_specs=P(("groups", "expert", "seq"), "tensor"),
        check_vma=False,
    )
```

```python
import jax
import jax.numpy as jnp
from jax import lax
from jax.experimental import pallas as pl
from jax.experimental.pallas import tpu as pltpu
from jax.sharding import PartitionSpec as P


def from_partner(value, axis, distance):
    mask = 2**distance
    pairs = [(source, source ^ mask) for source in range(lax.axis_size(axis))]
    return lax.ppermute(value, axis, pairs)


def expert_partial(block, gate_w, up_w, down_w):
    gate = jnp.einsum("...ecd,edf->...ecf", block, gate_w, preferred_element_type=jnp.float32)
    upper = jnp.einsum("...ecd,edf->...ecf", block, up_w, preferred_element_type=jnp.float32)
    hidden = (jax.nn.silu(gate) * upper).astype(jnp.bfloat16)
    return jnp.einsum("...ecf,efd->...ecd", hidden, down_w, preferred_element_type=jnp.float32)


def round_half(values):
    kept = lax.optimization_barrier(values.astype(jnp.bfloat16))
    return kept.astype(jnp.float32)


def slot_positions(keys, count):
    onehot = (keys[:, None] == jnp.arange(count, dtype=jnp.int32)[None, :]).astype(jnp.int32)
    before = jnp.cumsum(onehot, axis=0) - onehot
    return jnp.sum(before * onehot, axis=1)


def body(tokens, expert_ids, router_scores, w_gate, w_up, w_down):
    tok_rows, top = expert_ids.shape
    exp_dev = w_gate.shape[0]
    n_owner = lax.axis_size("expert")
    n_tensor = lax.axis_size("tensor")
    experts_all = exp_dev * n_owner * n_tensor
    slots = min(tok_rows, max(2, tok_rows * top * 2 // experts_all))
    buckets = n_owner * exp_dev
    shares = router_scores / jnp.sum(router_scores, axis=1, keepdims=True)
    flat_ids = expert_ids.reshape(-1)
    source_row = jnp.arange(tok_rows * top, dtype=jnp.int32) // top
    whole = lax.all_gather(tokens, "tensor", axis=1, tiled=True)
    column = lax.axis_index("tensor")
    mine = flat_ids // exp_dev % n_tensor == column
    bucket = flat_ids // (exp_dev * n_tensor) * exp_dev + flat_ids % exp_dev
    masked = jnp.where(mine, bucket, buckets)
    position = slot_positions(masked, buckets)
    target = jnp.where(mine, bucket * slots + position, buckets * slots)
    width = whole.shape[1]
    outgoing = (
        jnp.zeros((buckets * slots + 1, width), jnp.bfloat16).at[target].set(whole[source_row])
    )
    outgoing = outgoing[: buckets * slots].reshape(n_owner, exp_dev, slots, width)
    arrived = lax.all_to_all(outgoing, "expert", split_axis=0, concat_axis=0, tiled=True)
    other_gate, other_up, other_down = from_partner((w_gate, w_up, w_down), "seq", 0)
    own_part = expert_partial(arrived, w_gate, w_up, w_down)
    far_part = expert_partial(arrived, other_gate, other_up, other_down)
    answer = (own_part + round_half(far_part)).astype(jnp.bfloat16)
    back = lax.all_to_all(answer, "expert", split_axis=0, concat_axis=0, tiled=True)
    width = back.shape[-1]
    flat_back = jnp.concatenate(
        [back.reshape(buckets * slots, width), jnp.zeros((1, width), jnp.bfloat16)], axis=0
    )
    picked = flat_back[target].reshape(tok_rows, top, width)
    share_mine = jnp.where(mine.reshape(tok_rows, top), shares, 0.0)
    combined = jnp.sum(picked.astype(jnp.float32) * share_mine[:, :, None], axis=1)
    return lax.psum_scatter(combined, "tensor", scatter_dimension=1, tiled=True).astype(
        jnp.bfloat16
    )


def dense_kernel(
    tokens, ids, scores, gate_w, up_w, down_w, out,
    rows, tables, gate_all, up_all, down_all, hidden, part,
    diag, joined, side, final, back, send, recv, local,
):
    n_rows, cols = tokens.shape
    half = n_rows // 2
    units = gate_w.shape[2]
    z = lax.axis_index("expert")
    t = lax.axis_index("tensor")
    s = lax.axis_index("seq")
    tx, ty, td = t + 1 - 2 * (t % 2), (t + 2) % 4, 3 - t
    beside = ({"tensor": tx}, {"tensor": ty})
    along = (None, {"expert": z + 1 - 2 * (z % 2)}, {"expert": (z + 2) % 4}, {"expert": 3 - z})
    partner = {"seq": 1 - s}
    low, high, full = pl.ds(0, half), pl.ds(half, half), pl.ds(0, n_rows)

    def span(index):
        return pl.ds(pl.multiple_of(index * cols, cols), cols)

    barrier = pltpu.get_barrier_semaphore()
    for device in (partner,) + beside + along[1:]:
        pl.semaphore_signal(barrier, inc=1, device_id=device, device_id_type=pl.DeviceIdType.MESH)
    pl.semaphore_wait(barrier, 6)

    def remote(source, target, number, device):
        return pltpu.make_async_remote_copy(
            src_ref=source,
            dst_ref=target,
            send_sem=send.at[number],
            recv_sem=recv.at[number],
            device_id=device,
            device_id_type=pl.DeviceIdType.MESH,
        )

    mine = span(t)
    to_z = [None] + [remote(tokens, rows.at[j, :, mine], 2 + j, along[j]) for j in (1, 2, 3)]
    table_z = [None] + [remote(tables.at[0], tables.at[j], 5 + j, along[j]) for j in (1, 2, 3)]
    direct, passed, ahead, plain, summed = [], [], [], [], []
    for j in range(4):
        block = rows.at[j, :, mine]
        origin = tokens if j == 0 else block
        direct.append([remote(origin, block, 9 + 2 * j + d, beside[d]) for d in (0, 1)])
        passed.append([
            remote(rows.at[j, high, span(ty)], rows.at[j, high, span(ty)], 17 + 2 * j, beside[0]),
            remote(rows.at[j, low, span(tx)], rows.at[j, low, span(tx)], 18 + 2 * j, beside[1]),
        ])
        ahead.append([
            remote(part.at[j, low, span(td)], diag.at[j, 0], 25 + 2 * j, beside[0]),
            remote(part.at[j, high, span(td)], diag.at[j, 1], 26 + 2 * j, beside[1]),
        ])
        plain.append([
            remote(part.at[j, low, span(tx)], side.at[j, 0, low], 33 + 2 * j, beside[0]),
            remote(part.at[j, high, span(ty)], side.at[j, 1, high], 34 + 2 * j, beside[1]),
        ])
        summed.append([
            remote(joined.at[j, 0], side.at[j, 0, high], 41 + 2 * j, beside[0]),
            remote(joined.at[j, 1], side.at[j, 1, low], 42 + 2 * j, beside[1]),
        ])
    relay = [
        remote(rows.at[0, :, span(index)], rows.at[1, :, span(index)], 52 + i, along[1])
        for i, index in enumerate((tx, ty, td))
    ]
    to_home = [None] + [remote(final.at[j], back.at[j], 48 + j, along[j]) for j in (1, 2, 3)]
    weights = [
        remote(gate_w.at[0], gate_all.at[:, pl.ds(units, units)], 0, partner),
        remote(up_w.at[0], up_all.at[:, pl.ds(units, units)], 1, partner),
        remote(down_w.at[0], down_all.at[pl.ds(units, units)], 2, partner),
    ]
    loads = [
        pltpu.make_async_copy(tokens, rows.at[0, :, mine], local.at[0]),
        pltpu.make_async_copy(gate_w.at[0], gate_all.at[:, pl.ds(0, units)], local.at[1]),
        pltpu.make_async_copy(up_w.at[0], up_all.at[:, pl.ds(0, units)], local.at[2]),
        pltpu.make_async_copy(down_w.at[0], down_all.at[pl.ds(0, units)], local.at[3]),
    ]

    def start(copies):
        for copy in copies:
            copy.start()

    def arrive(copies):
        for copy in copies:
            copy.wait_recv()

    def spread(j):
        to_z[j].wait_recv()
        start(direct[j])

    def pass_on(j):
        arrive(direct[j])
        start(passed[j])
        if j == 0:
            start(relay[:2])

    def answer(j, sending):
        arrive(to_z[1:2] + relay if j == 1 else passed[j])
        if j == 0:
            start(relay[2:])

        def inner(c, carry):
            at = pl.ds(pl.multiple_of(c * 256, 256), 256)
            gate = jnp.dot(rows[j], gate_all[:, at], preferred_element_type=jnp.float32)
            upper = jnp.dot(rows[j], up_all[:, at], preferred_element_type=jnp.float32)
            hidden[:, at] = (gate * jax.nn.sigmoid(gate) * upper).astype(jnp.bfloat16)
            return carry

        lax.fori_loop(0, 2 * units // 256, inner, 0)
        share = tables[j, pl.ds(z * 4 + t, 1), :]
        share = jnp.broadcast_to(share, (128, n_rows)).T[:, :1]
        for index, copies in ((td, ahead[j]), (tx, plain[j][:1]), (ty, plain[j][1:]), (t, [])):
            value = jnp.dot(hidden[...], down_all[:, span(index)], preferred_element_type=jnp.float32)
            part[j, :, span(index)] = (value * share).astype(jnp.bfloat16)
            if sending:
                start(copies)

    def join(j):
        arrive(ahead[j])
        upper_rows = part[j, high, span(tx)].astype(jnp.float32) + diag[j, 1].astype(jnp.float32)
        joined[j, 0] = upper_rows.astype(jnp.bfloat16)
        lower_rows = part[j, low, span(ty)].astype(jnp.float32) + diag[j, 0].astype(jnp.float32)
        joined[j, 1] = lower_rows.astype(jnp.bfloat16)
        start(summed[j])

    def gathered(j):
        arrive(plain[j] + summed[j])
        return (
            part[j, :, mine].astype(jnp.float32)
            + side[j, 0].astype(jnp.float32)
            + side[j, 1].astype(jnp.float32)
        )

    def go_home(j):
        final[j] = gathered(j).astype(jnp.bfloat16)
        to_home[j].start()

    start(direct[0])
    start(to_z[2:] + to_z[1:2])
    start(weights)
    start(loads)
    shares = scores[...] / jnp.sum(scores[...], axis=0, keepdims=True)
    number = lax.broadcasted_iota(jnp.int32, (16, n_rows), 0)
    table = jnp.zeros((16, n_rows), jnp.float32)
    for k in range(ids.shape[0]):
        table = table + jnp.where(ids[k : k + 1, :] == number, shares[k : k + 1, :], 0.0)
    tables[0] = table
    start(table_z[1:])
    pass_on(0)
    spread(2)
    for copy in loads:
        copy.wait()
    arrive(weights + table_z[1:])
    answer(0, False)
    pass_on(2)
    spread(3)
    answer(2, True)
    pass_on(3)
    answer(1, True)
    join(2)
    start(ahead[0] + plain[0])
    answer(3, True)
    join(1)
    go_home(2)
    join(3)
    go_home(1)
    join(0)
    go_home(3)
    total = gathered(0)
    arrive(to_home[1:])
    for j in (1, 2, 3):
        total = total + back[j].astype(jnp.float32)
    out[...] = total.astype(jnp.bfloat16)
    everything = to_z[1:] + relay + table_z[1:] + weights + to_home[1:]
    for group in direct[:1] + direct[2:] + passed[:1] + passed[2:] + ahead + plain + summed:
        everything = everything + group
    for copy in everything:
        copy.wait_send()


def dense_body(tokens, expert_ids, router_scores, w_gate, w_up, w_down):
    n_rows, cols = tokens.shape
    _, width, units = w_gate.shape
    half = n_rows // 2
    bf16 = jnp.bfloat16
    return pl.pallas_call(
        dense_kernel,
        out_shape=jax.ShapeDtypeStruct((n_rows, cols), bf16),
        in_specs=[pl.BlockSpec(memory_space=pltpu.HBM)]
        + [pl.BlockSpec(memory_space=pltpu.VMEM)] * 2
        + [pl.BlockSpec(memory_space=pltpu.HBM)] * 3,
        out_specs=pl.BlockSpec(memory_space=pltpu.VMEM),
        scratch_shapes=[
            pltpu.VMEM((4, n_rows, width), bf16),
            pltpu.VMEM((4, 16, n_rows), jnp.float32),
            pltpu.VMEM((width, 2 * units), bf16),
            pltpu.VMEM((width, 2 * units), bf16),
            pltpu.VMEM((2 * units, width), bf16),
            pltpu.VMEM((n_rows, 2 * units), bf16),
            pltpu.VMEM((4, n_rows, width), bf16),
            pltpu.VMEM((4, 2, half, cols), bf16),
            pltpu.VMEM((4, 2, half, cols), bf16),
            pltpu.VMEM((4, 2, n_rows, cols), bf16),
            pltpu.VMEM((4, n_rows, cols), bf16),
            pltpu.VMEM((4, n_rows, cols), bf16),
            pltpu.SemaphoreType.DMA((55,)),
            pltpu.SemaphoreType.DMA((55,)),
            pltpu.SemaphoreType.DMA((4,)),
        ],
        compiler_params=pltpu.CompilerParams(
            collective_id=0, has_side_effects=True, vmem_limit_bytes=62 * 1024 * 1024
        ),
        cost_estimate=pl.CostEstimate(
            flops=4 * n_rows * 6 * width * 2 * units,
            bytes_accessed=6 * width * units * 2,
            transcendentals=4 * n_rows * 2 * units,
        ),
    )(tokens, expert_ids.T, router_scores.T, w_gate, w_up, w_down)


def pick_body(tokens, expert_ids, router_scores, w_gate, w_up, w_down):
    tok_rows, top = expert_ids.shape
    exp_dev = w_gate.shape[0]
    n_owner, n_tensor = lax.axis_size("expert"), lax.axis_size("tensor")
    slots = min(tok_rows, max(2, tok_rows * top * 2 // (exp_dev * n_owner * n_tensor)))
    dense = exp_dev == 1 and n_owner == 4 and n_tensor == 4 and slots == tok_rows
    plan = dense_body if dense else body
    return plan(tokens, expert_ids, router_scores, w_gate, w_up, w_down)


def solution(mesh):
    placed = (
        P(("groups", "expert", "seq"), "tensor"),
        P(("groups", "expert", "seq"), None),
        P(("groups", "expert", "seq"), None),
        P(("expert", "tensor"), None, "seq"),
        P(("expert", "tensor"), None, "seq"),
        P(("expert", "tensor"), "seq", None),
    )
    return jax.shard_map(
        pick_body,
        mesh=mesh,
        in_specs=placed,
        out_specs=P(("groups", "expert", "seq"), "tensor"),
        check_vma=False,
    )
```
